32 devices in a mesh: seq: 8 (over z, x), tp: 4 (over y, core).
Axes of the slice: x: 2, y: 2, z: 4, core: 2. Of those that a mesh axis runs over, the one named last changes fastest.
Arguments:
- streams: bfloat16 [3, 4096, 2048], P(None, 'seq', 'tp'), may hold values from -6 to 6
- short_taps: float32 [3, 3, 2048], P(None, None, 'tp'), may hold values from -3 to 3
- filter_taps: float32 [4096, 2048], P('seq', 'tp'), may hold values from -0.09375 to 0.09375
- skip_gain: float32 [2048], P('tp'), may hold values from -4 to 4
- w_out: bfloat16 [2048, 4096], P('tp'), may hold values from -0.1875 to 0.1875
- cotangent: bfloat16 [4096, 4096], P('seq'), may hold values from -6 to 6
Outputs:
- mixed: bfloat16 [4096, 4096], P('seq', 'tp')
- stream_grads: bfloat16 [3, 4096, 2048], P(None, 'seq', 'tp')
The draws below stay inside these ranges and needn't reach their ends.
All inputs are finite; a program needn't handle non-finite values.
Results may differ from the reference program's by a relative error of at most 0.005.
Values may be sent and summed in bfloat16 or wider, within the bound.
A program may use at most 128 MiB of HBM per device.

```python
import jax
import jax.numpy as jnp

D = 4096
C = 2048
L = 4096


def raised(result, stream_key, source, target, shards_of, factor):
    def block_of(position):
        return (jnp.arange(result.shape[position]) // (result.shape[position] // shards_of)).reshape((-1,) + (1,) * (result.ndim - 1 - position))

    one_side = jax.random.permutation(stream_key, shards_of)[block_of(target)]
    second = (block_of(target) + shards_of // 2) % shards_of
    return jnp.where((block_of(source) == one_side) | (block_of(source) == second), factor * result, result)


def block_levels(rng, dims, split, least, largest):
    level, own = 1.0, jax.random.fold_in(rng, 6)
    for dim, shards_of in split:
        draws = jnp.exp(jax.random.uniform(jax.random.fold_in(own, dim), (shards_of,), jnp.float32, least / len(split), largest / len(split)))
        level = level * jnp.repeat(draws, dims[dim] // shards_of).reshape([-1 if axis == dim else 1 for axis in range(len(dims))])
    return level


def normal_values(key, dims, deviation, most, cuts=(), kind=jnp.bfloat16):
    factor_of = block_levels(key, dims, cuts, -0.22, 0.18) if cuts else 1.0
    array = jax.random.normal(key, dims, jnp.float32) * deviation * factor_of
    return jnp.minimum(jnp.maximum(array, -most), most).astype(kind)


def heavy_noise(key, extent, scale, reach, cuts, heavy, kind=jnp.bfloat16):
    drawn = scale * jax.random.normal(key, extent, jnp.float32)
    if cuts:
        drawn = drawn * block_levels(key, extent, cuts, -0.22, 0.18)
    return jnp.clip(raised(drawn, jax.random.fold_in(key, 3), *heavy), -reach, reach).astype(kind)


def setup_inputs(seed: int = 0) -> dict:
    keys = jax.random.split(jax.random.key(seed), 7)
    return {
        "streams": normal_values(keys[0], (3, L, C), 1.0, 6.0, ((1, 8), (2, 4))),
        "short_taps": normal_values(keys[1], (3, 3, C), 0.6, 3.0, ((2, 4),), jnp.float32),
        "filter_taps": normal_values(keys[2], (L, C), L ** -0.5, 0.09375, ((0, 8), (1, 4)), jnp.float32),
        "skip_gain": normal_values(keys[3], (C,), 1.0, 4.0, ((0, 4),), jnp.float32),
        "w_out": heavy_noise(keys[4], (C, D), C ** -0.5, 0.1875, ((0, 4),), (0, 1, 4, 2.0)),
        "cotangent": normal_values(keys[5], (L, D), 1.0, 6.0, ((0, 8),)),
    }


def causal_taps(stream, taps):
    padded = jnp.pad(stream, ((2, 0), (0, 0)))
    return taps[0] * padded[2:] + taps[1] * padded[1:-1] + taps[2] * padded[:-2]


def ahead_taps(gradient, taps):
    padded = jnp.pad(gradient, ((0, 2), (0, 0)))
    return taps[0] * padded[:-2] + taps[1] * padded[1:-1] + taps[2] * padded[2:]


def reference(streams, short_taps, filter_taps, skip_gain, w_out, cotangent):
    length = streams.shape[1]
    points = 2 * length
    values = streams.astype(jnp.float32)
    conv_q = causal_taps(values[0], short_taps[0])
    conv_k = causal_taps(values[1], short_taps[1])
    conv_v = causal_taps(values[2], short_taps[2])
    source = conv_k * conv_v
    kernel = jnp.fft.rfft(filter_taps, n=points, axis=0)
    long_part = jnp.fft.irfft(kernel * jnp.fft.rfft(source, n=points, axis=0), n=points, axis=0)[:length]
    mixer_state = long_part + skip_gain * source
    gated = (conv_q * mixer_state).astype(jnp.bfloat16)
    mixed = jnp.dot(gated, w_out, preferred_element_type=jnp.float32).astype(jnp.bfloat16)
    grad_gated = jnp.dot(cotangent, w_out.T, preferred_element_type=jnp.float32)
    grad_q = grad_gated * mixer_state
    grad_state = grad_gated * conv_q
    grad_long = jnp.fft.irfft(jnp.conj(kernel) * jnp.fft.rfft(grad_state, n=points, axis=0), n=points, axis=0)[:length]
    grad_source = grad_long + skip_gain * grad_state
    grad_k = grad_source * conv_v
    grad_v = grad_source * conv_k
    stream_grads = jnp.stack([
        ahead_taps(grad_q, short_taps[0]),
        ahead_taps(grad_k, short_taps[1]),
        ahead_taps(grad_v, short_taps[2]),
    ]).astype(jnp.bfloat16)
    return mixed, stream_grads
```

```python
import functools
import math

import jax
import jax.numpy as jnp
import ml_dtypes
import numpy as np
from jax import lax
from jax.experimental import pallas as pl
from jax.experimental.pallas import tpu as pltpu
from jax.sharding import PartitionSpec as P


def passed_along(x, axis, by):
    devices = lax.axis_size(axis)
    pairs = [(i, i + by) for i in range(devices) if 0 <= i + by < devices]
    return lax.ppermute(x, axis, pairs)


def dft_tables(length):
    ids = np.arange(length)
    angles = (np.outer(ids, ids) % length) * (2.0 * math.pi / length)
    cosine, sine = np.cos(angles), np.sin(angles)
    table = np.block([[cosine, -sine], [sine, cosine]]).astype(np.float32)
    high = table.astype(ml_dtypes.bfloat16)
    low = (table - high.astype(np.float32)).astype(ml_dtypes.bfloat16)
    return high, low


def twiddle_table(devices, length):
    angles = -2.0 * math.pi * np.outer(np.arange(devices) + 0.25, np.arange(length)) / (devices * length)
    return np.stack([np.cos(angles), np.sin(angles)]).astype(np.float32)


def across_weights(devices):
    angles = -2.0 * math.pi * np.outer(np.arange(devices) + 0.25, np.arange(devices)) / devices
    return np.cos(angles), np.sin(angles)


def split_store(high_ref, low_ref, rows, lanes, value):
    high = value.astype(jnp.bfloat16)
    high_ref[rows, lanes] = high
    low_ref[rows, lanes] = (value - high.astype(jnp.float32)).astype(jnp.bfloat16)


row_step = 16
lane_step = 128


def tiles_of(channels, length, body):
    per_row = length // lane_step

    @pl.loop(0, (channels // row_step) * per_row)
    def _(step):
        row = pl.multiple_of((step // per_row) * row_step, row_step)
        lane = pl.multiple_of((step % per_row) * lane_step, lane_step)
        body(row, lane)


def forward_across(x_ref, twiddle_ref, high_ref, low_ref):
    devices, channels, length = x_ref.shape
    real_w, imag_w = across_weights(devices)

    def body(row, lane):
        lanes = pl.ds(lane, lane_step)
        values = [x_ref[m, pl.ds(row, row_step), lanes].astype(jnp.float32) for m in range(devices)]
        for k in range(devices):
            real = values[0] * float(real_w[k, 0])
            imag = None
            for m in range(1, devices):
                real = real + values[m] * float(real_w[k, m])
                term = values[m] * float(imag_w[k, m])
                imag = term if imag is None else imag + term
            twiddle_real = twiddle_ref[0, pl.ds(k, 1), lanes]
            twiddle_imag = twiddle_ref[1, pl.ds(k, 1), lanes]
            rows = pl.ds(pl.multiple_of(k * channels + row, row_step), row_step)
            split_store(high_ref, low_ref, rows, lanes, real * twiddle_real - imag * twiddle_imag)
            upper = pl.ds(pl.multiple_of(length + lane, lane_step), lane_step)
            split_store(high_ref, low_ref, rows, upper, real * twiddle_imag + imag * twiddle_real)

    tiles_of(channels, length, body)


def transform(high_ref, low_ref, table_high_ref, table_low_ref, out_ref):
    width = out_ref.shape[1]
    part = 256

    @pl.loop(0, width // part)
    def _(step):
        lanes = pl.ds(pl.multiple_of(step * part, part), part)
        dot = functools.partial(jnp.dot, preferred_element_type=jnp.float32)
        out_ref[:, lanes] = (
            dot(high_ref[...], table_high_ref[:, lanes])
            + dot(low_ref[...], table_high_ref[:, lanes])
            + dot(high_ref[...], table_low_ref[:, lanes])
        )


def spectrum_kernel(x_ref, twiddle_ref, table_high_ref, table_low_ref, out_ref, high_ref, low_ref):
    forward_across(x_ref, twiddle_ref, high_ref, low_ref)
    transform(high_ref, low_ref, table_high_ref, table_low_ref, out_ref)


def filter_kernel(sign, x_ref, spectrum_ref, twiddle_ref, table_high_ref, table_low_ref, out_ref, high_ref, low_ref, full_ref):
    devices, channels, length = x_ref.shape
    forward_across(x_ref, twiddle_ref, high_ref, low_ref)
    transform(high_ref, low_ref, table_high_ref, table_low_ref, full_ref)
    real_w, imag_w = across_weights(devices)
    scale = 1.0 / (devices * length)

    def multiply(row, lane):
        rows = pl.ds(row, row_step)
        lanes = pl.ds(lane, lane_step)
        upper = pl.ds(pl.multiple_of(length + lane, lane_step), lane_step)
        data_real, data_imag = full_ref[rows, lanes], full_ref[rows, upper]
        taps_real, taps_imag = spectrum_ref[rows, lanes], spectrum_ref[rows, upper] * sign
        split_store(high_ref, low_ref, rows, lanes, data_real * taps_real - data_imag * taps_imag)
        split_store(high_ref, low_ref, rows, upper, -(data_real * taps_imag + data_imag * taps_real))

    tiles_of(devices * channels, length, multiply)
    transform(high_ref, low_ref, table_high_ref, table_low_ref, full_ref)

    def inverse(row, lane):
        lanes = pl.ds(lane, lane_step)
        upper = pl.ds(pl.multiple_of(length + lane, lane_step), lane_step)
        sums = [None] * devices
        for k in range(devices):
            rows = pl.ds(pl.multiple_of(k * channels + row, row_step), row_step)
            twiddle_real = twiddle_ref[0, pl.ds(k, 1), lanes]
            twiddle_imag = twiddle_ref[1, pl.ds(k, 1), lanes]
            real, imag = full_ref[rows, lanes], full_ref[rows, upper]
            turned_real = real * twiddle_real - imag * twiddle_imag
            turned_imag = real * twiddle_imag + imag * twiddle_real
            for m in range(devices):
                term = turned_real * float(scale * real_w[k, m])
                if m:
                    term = term - turned_imag * float(scale * imag_w[k, m])
                sums[m] = term if sums[m] is None else sums[m] + term
        for m in range(devices):
            out_ref[m, pl.ds(row, row_step), lanes] = sums[m].astype(jnp.bfloat16)

    tiles_of(channels, length, inverse)


def tables_for(devices, length):
    high, low = dft_tables(length)
    return jnp.asarray(twiddle_table(devices, length)), jnp.asarray(high), jnp.asarray(low)


def spectrum(x, tables):
    devices, channels, length = x.shape
    rows = devices * channels
    return pl.pallas_call(
        spectrum_kernel,
        out_shape=jax.ShapeDtypeStruct((rows, 2 * length), jnp.float32),
        scratch_shapes=[pltpu.VMEM((rows, 2 * length), jnp.bfloat16)] * 2,
        compiler_params=pltpu.CompilerParams(vmem_limit_bytes=40 << 20),
        cost_estimate=pl.CostEstimate(
            flops=6 * rows * (2 * length) ** 2, bytes_accessed=8 << 20, transcendentals=0
        ),
    )(x, *tables)


def filtered(x, taps_spectrum, tables, sign):
    devices, channels, length = x.shape
    rows = devices * channels
    return pl.pallas_call(
        functools.partial(filter_kernel, sign),
        out_shape=jax.ShapeDtypeStruct(x.shape, jnp.bfloat16),
        scratch_shapes=[pltpu.VMEM((rows, 2 * length), jnp.bfloat16)] * 2
        + [pltpu.VMEM((rows, 2 * length), jnp.float32)],
        compiler_params=pltpu.CompilerParams(vmem_limit_bytes=40 << 20),
        cost_estimate=pl.CostEstimate(
            flops=12 * rows * (2 * length) ** 2, bytes_accessed=8 << 20, transcendentals=0
        ),
    )(x, taps_spectrum, *tables)


def to_channels(x):
    devices = lax.axis_size("seq")
    turned = x.astype(jnp.bfloat16).T
    moved = lax.all_to_all(turned, "seq", split_axis=0, concat_axis=0, tiled=True)
    return moved.reshape(devices, x.shape[1] // devices, x.shape[0])


def to_positions(x):
    devices, channels, length = x.shape
    moved = lax.all_to_all(x.reshape(devices * channels, length), "seq", split_axis=0, concat_axis=0, tiled=True)
    return moved.T.astype(jnp.float32)


def on_device(streams, short_taps, filter_taps, skip_gain, w_out, cotangent):
    length = streams.shape[1]
    devices = lax.axis_size("seq")
    tables = tables_for(devices, length)
    taps_channels = to_channels(filter_taps)
    previous = passed_along(streams[:, -2:, :], "seq", 1)
    extended = jnp.concatenate([previous, streams], axis=1).astype(jnp.float32)
    convolved = (
        short_taps[:, 0, None, :] * extended[:, 2:]
        + short_taps[:, 1, None, :] * extended[:, 1:-1]
        + short_taps[:, 2, None, :] * extended[:, :-2]
    )
    conv_q = convolved[0]
    conv_k = convolved[1]
    conv_v = convolved[2]
    source = conv_k * conv_v
    grad_gated = lax.dot_general(
        cotangent, w_out, (((1,), (1,)), ((), ())), preferred_element_type=jnp.float32
    )
    grad_state = grad_gated * conv_q
    w_columns = lax.all_to_all(w_out, "tp", split_axis=1, concat_axis=0, tiled=True)
    taps_spectrum = spectrum(taps_channels, tables)
    mixer_state = to_positions(filtered(to_channels(source), taps_spectrum, tables, 1.0)) + skip_gain * source
    gated = (conv_q * mixer_state).astype(jnp.bfloat16)
    all_gated = lax.all_gather(gated, "tp", axis=1, tiled=True)
    mixed = jnp.dot(all_gated, w_columns, preferred_element_type=jnp.float32).astype(jnp.bfloat16)
    grad_q = grad_gated * mixer_state
    grad_source = to_positions(filtered(to_channels(grad_state), taps_spectrum, tables, -1.0)) + skip_gain * grad_state
    gradients = jnp.stack([grad_q, grad_source * conv_v, grad_source * conv_k])
    following = passed_along(gradients[:, :2, :], "seq", -1)
    grad_ext = jnp.concatenate([gradients, following], axis=1)
    stream_grads = (
        short_taps[:, 0, None, :] * grad_ext[:, :-2]
        + short_taps[:, 1, None, :] * grad_ext[:, 1:-1]
        + short_taps[:, 2, None, :] * grad_ext[:, 2:]
    )
    return (mixed, stream_grads.astype(jnp.bfloat16))


def solution(mesh):
    return jax.shard_map(
        on_device,
        mesh=mesh,
        in_specs=(
            P(None, "seq", "tp"),
            P(None, None, "tp"),
            P("seq", "tp"),
            P("tp"),
            P("tp", None),
            P("seq", None),
        ),
        out_specs=(P("seq", "tp"), P(None, "seq", "tp")),
        check_vma=False,
    )
```

```python
import functools
import math

import jax
import jax.numpy as jnp
import ml_dtypes
import numpy as np
from jax import lax
from jax.experimental import pallas as pl
from jax.experimental.pallas import tpu as pltpu
from jax.sharding import PartitionSpec as P


def passed_along(x, axis, by):
    devices = lax.axis_size(axis)
    pairs = [(i, i + by) for i in range(devices) if 0 <= i + by < devices]
    return lax.ppermute(x, axis, pairs)


def dft_tables(length):
    ids = np.arange(length)
    angles = (np.outer(ids, ids) % length) * (2.0 * math.pi / length)
    cosine, sine = np.cos(angles), np.sin(angles)
    table = np.block([[cosine, -sine], [sine, cosine]]).astype(np.float32)
    high = table.astype(ml_dtypes.bfloat16)
    low = (table - high.astype(np.float32)).astype(ml_dtypes.bfloat16)
    return high, low


def twiddle_table(devices, length):
    angles = -2.0 * math.pi * np.outer(np.arange(devices) + 0.25, np.arange(length)) / (devices * length)
    return np.stack([np.cos(angles), np.sin(angles)]).astype(np.float32)


def across_weights(devices):
    angles = -2.0 * math.pi * np.outer(np.arange(devices) + 0.25, np.arange(devices)) / devices
    return np.cos(angles), np.sin(angles)


def split_store(high_ref, low_ref, rows, lanes, value):
    high = value.astype(jnp.bfloat16)
    high_ref[rows, lanes] = high
    low_ref[rows, lanes] = (value - high.astype(jnp.float32)).astype(jnp.bfloat16)


row_step = 16
lane_step = 128


def tiles_of(channels, length, body):
    per_row = length // lane_step

    @pl.loop(0, (channels // row_step) * per_row)
    def _(step):
        row = pl.multiple_of((step // per_row) * row_step, row_step)
        lane = pl.multiple_of((step % per_row) * lane_step, lane_step)
        body(row, lane)


def complex_sum(values, real_weights, imag_weights):
    real = imag = None
    for value, real_w, imag_w in zip(values, real_weights, imag_weights):
        real_term, imag_term = value * float(real_w), value * float(imag_w)
        real = real_term if real is None else real + real_term
        imag = imag_term if imag is None else imag + imag_term
    return real, imag


def forward_across(x_ref, twiddle_ref, high_ref, low_ref):
    devices, channels, length = x_ref.shape
    half = devices // 2
    real_w, imag_w = across_weights(devices)

    def body(row, lane):
        lanes = pl.ds(lane, lane_step)
        upper = pl.ds(pl.multiple_of(length + lane, lane_step), lane_step)
        values = [x_ref[m, pl.ds(row, row_step), lanes].astype(jnp.float32) for m in range(devices)]
        for k in range(half):
            even = complex_sum(values[::2], real_w[k, ::2], imag_w[k, ::2])
            odd = complex_sum(values[1::2], real_w[k, 1::2], imag_w[k, 1::2])
            for at, real, imag in (
                (k, even[0] + odd[0], even[1] + odd[1]),
                (k + half, even[0] - odd[0], even[1] - odd[1]),
            ):
                twiddle_real = twiddle_ref[0, pl.ds(at, 1), lanes]
                twiddle_imag = twiddle_ref[1, pl.ds(at, 1), lanes]
                rows = pl.ds(pl.multiple_of(at * channels + row, row_step), row_step)
                split_store(high_ref, low_ref, rows, lanes, real * twiddle_real - imag * twiddle_imag)
                split_store(high_ref, low_ref, rows, upper, real * twiddle_imag + imag * twiddle_real)

    tiles_of(channels, length, body)


def transform(high_ref, low_ref, table_high_ref, table_low_ref, out_ref):
    width = out_ref.shape[1]
    part = 256

    @pl.loop(0, width // part)
    def _(step):
        lanes = pl.ds(pl.multiple_of(step * part, part), part)
        dot = functools.partial(jnp.dot, preferred_element_type=jnp.float32)
        out_ref[:, lanes] = (
            dot(high_ref[...], table_high_ref[:, lanes])
            + dot(low_ref[...], table_high_ref[:, lanes])
            + dot(high_ref[...], table_low_ref[:, lanes])
        )


def table_copies(table_refs, held_refs, sems):
    copies = [
        pltpu.make_async_copy(table, held, sems.at[i])
        for i, (table, held) in enumerate(zip(table_refs, held_refs))
    ]
    for copy in copies:
        copy.start()
    return copies


def spectrum_kernel(x_ref, twiddle_ref, table_high, table_low, out_ref, held_high, held_low, sems, high_ref, low_ref):
    copies = table_copies((table_high, table_low), (held_high, held_low), sems)
    forward_across(x_ref, twiddle_ref, high_ref, low_ref)
    for copy in copies:
        copy.wait()
    transform(high_ref, low_ref, held_high, held_low, out_ref)


def filter_kernel(
    sign, x_ref, twiddle_ref, table_high, table_low, spectrum_hbm, out_ref,
    held_high, held_low, spectrum_ref, sems, high_ref, low_ref, full_ref,
):
    devices, channels, length = x_ref.shape
    half = devices // 2
    copies = table_copies(
        (table_high, table_low, spectrum_hbm), (held_high, held_low, spectrum_ref), sems
    )
    forward_across(x_ref, twiddle_ref, high_ref, low_ref)
    for copy in copies:
        copy.wait()
    transform(high_ref, low_ref, held_high, held_low, full_ref)
    real_w, imag_w = across_weights(devices)
    scale = 1.0 / (devices * length)

    @pl.loop(0, devices * channels // row_step)
    def _(step):
        rows = pl.ds(pl.multiple_of(step * row_step, row_step), row_step)
        for lane in range(0, length, lane_step):
            lanes, upper = pl.ds(lane, lane_step), pl.ds(length + lane, lane_step)
            data_real, data_imag = full_ref[rows, lanes], full_ref[rows, upper]
            taps_real, taps_imag = spectrum_ref[rows, lanes], spectrum_ref[rows, upper] * sign
            split_store(high_ref, low_ref, rows, lanes, data_real * taps_real - data_imag * taps_imag)
            split_store(high_ref, low_ref, rows, upper, -(data_real * taps_imag + data_imag * taps_real))

    transform(high_ref, low_ref, held_high, held_low, full_ref)

    def inverse(row, lane):
        lanes = pl.ds(lane, lane_step)
        upper = pl.ds(pl.multiple_of(length + lane, lane_step), lane_step)
        sums = [None] * devices
        for k in range(half):
            turned = []
            for at in (k, k + half):
                rows = pl.ds(pl.multiple_of(at * channels + row, row_step), row_step)
                twiddle_real = twiddle_ref[0, pl.ds(at, 1), lanes]
                twiddle_imag = twiddle_ref[1, pl.ds(at, 1), lanes]
                real, imag = full_ref[rows, lanes], full_ref[rows, upper]
                turned.append((real * twiddle_real - imag * twiddle_imag, real * twiddle_imag + imag * twiddle_real))
            (near_real, near_imag), (far_real, far_imag) = turned
            even = (near_real + far_real, near_imag + far_imag)
            odd = (near_real - far_real, near_imag - far_imag)
            for m in range(devices):
                real, imag = odd if m % 2 else even
                term = real * float(scale * real_w[k, m]) - imag * float(scale * imag_w[k, m])
                sums[m] = term if sums[m] is None else sums[m] + term
        for m in range(devices):
            out_ref[m, pl.ds(row, row_step), lanes] = sums[m].astype(jnp.bfloat16)

    tiles_of(channels, length, inverse)


def tables_for(devices, length):
    high, low = dft_tables(length)
    return jnp.asarray(twiddle_table(devices, length)), jnp.asarray(high), jnp.asarray(low)


in_vmem = pl.BlockSpec(memory_space=pltpu.VMEM)
in_hbm = pl.BlockSpec(memory_space=pltpu.HBM)


def spectrum(x, tables):
    devices, channels, length = x.shape
    rows, width = devices * channels, 2 * length
    return pl.pallas_call(
        spectrum_kernel,
        out_shape=jax.ShapeDtypeStruct((rows, width), jnp.float32),
        in_specs=[in_vmem, in_vmem, in_hbm, in_hbm],
        out_specs=in_vmem,
        scratch_shapes=[pltpu.VMEM((width, width), jnp.bfloat16)] * 2
        + [pltpu.SemaphoreType.DMA((2,))]
        + [pltpu.VMEM((rows, width), jnp.bfloat16)] * 2,
        compiler_params=pltpu.CompilerParams(vmem_limit_bytes=40 << 20),
        cost_estimate=pl.CostEstimate(flops=6 * rows * width**2, bytes_accessed=8 << 20, transcendentals=0),
    )(x, *tables)


def filtered(x, taps_spectrum, tables, sign):
    devices, channels, length = x.shape
    rows, width = devices * channels, 2 * length
    return pl.pallas_call(
        functools.partial(filter_kernel, sign),
        out_shape=jax.ShapeDtypeStruct(x.shape, jnp.bfloat16),
        in_specs=[in_vmem, in_vmem, in_hbm, in_hbm, in_hbm],
        out_specs=in_vmem,
        scratch_shapes=[pltpu.VMEM((width, width), jnp.bfloat16)] * 2
        + [pltpu.VMEM((rows, width), jnp.float32), pltpu.SemaphoreType.DMA((3,))]
        + [pltpu.VMEM((rows, width), jnp.bfloat16)] * 2
        + [pltpu.VMEM((rows, width), jnp.float32)],
        compiler_params=pltpu.CompilerParams(vmem_limit_bytes=40 << 20),
        cost_estimate=pl.CostEstimate(flops=12 * rows * width**2, bytes_accessed=8 << 20, transcendentals=0),
    )(x, *tables, taps_spectrum)


def swapped(x, axis, bit):
    return lax.ppermute(x, axis, [(i, i ^ bit) for i in range(lax.axis_size(axis))])


def to_channels(x):
    devices = lax.axis_size("seq")
    turned = x.astype(jnp.bfloat16).T
    moved = lax.all_to_all(turned, "seq", split_axis=0, concat_axis=0, tiled=True)
    return moved.reshape(devices, x.shape[1] // devices, x.shape[0])


def to_positions(x):
    devices, channels, length = x.shape
    moved = lax.all_to_all(x.reshape(devices * channels, length), "seq", split_axis=0, concat_axis=0, tiled=True)
    return moved.T.astype(jnp.float32)


def on_device(streams, short_taps, filter_taps, skip_gain, w_out, cotangent):
    length = streams.shape[1]
    devices = lax.axis_size("seq")
    tables = tables_for(devices, length)
    taps_channels = to_channels(filter_taps)
    previous = passed_along(streams[:, -2:, :], "seq", 1)
    extended = jnp.concatenate([previous, streams], axis=1).astype(jnp.float32)
    convolved = (
        short_taps[:, 0, None, :] * extended[:, 2:]
        + short_taps[:, 1, None, :] * extended[:, 1:-1]
        + short_taps[:, 2, None, :] * extended[:, :-2]
    )
    conv_q = convolved[0]
    conv_k = convolved[1]
    conv_v = convolved[2]
    source = conv_k * conv_v
    grad_gated = lax.dot_general(
        cotangent, w_out, (((1,), (1,)), ((), ())), preferred_element_type=jnp.float32
    )
    grad_state = grad_gated * conv_q
    shares = lax.axis_size("tp")
    place = lax.axis_index("tp")
    width = w_out.shape[1] // shares
    w_pieces = []
    for bits in range(shares):
        piece = lax.dynamic_slice_in_dim(w_out, (place ^ bits) * width, width, 1)
        w_pieces.append(swapped(piece, "tp", bits) if bits else piece)
    taps_spectrum = spectrum(taps_channels, tables)
    state_channels = filtered(to_channels(source), taps_spectrum, tables, 1.0)
    grad_channels, w_pieces = lax.optimization_barrier((to_channels(grad_state), w_pieces))
    mixer_state = to_positions(state_channels) + skip_gain * source
    gated = (conv_q * mixer_state).astype(jnp.bfloat16)
    pieces = {0: gated}
    bit = shares // 2
    while bit:
        order = sorted(pieces)
        received = swapped(jnp.stack([pieces[i] for i in order]), "tp", bit)
        pieces.update({i ^ bit: received[at] for at, i in enumerate(order)})
        bit //= 2
    total = sum(
        jnp.dot(pieces[i], w_pieces[i], preferred_element_type=jnp.float32) for i in range(shares)
    )
    mixed = total.astype(jnp.bfloat16)
    grad_q = grad_gated * mixer_state
    grad_source = to_positions(filtered(grad_channels, taps_spectrum, tables, -1.0)) + skip_gain * grad_state
    gradients = jnp.stack([grad_q, grad_source * conv_v, grad_source * conv_k])
    following = passed_along(gradients[:, :2, :], "seq", -1)
    grad_ext = jnp.concatenate([gradients, following], axis=1)
    stream_grads = (
        short_taps[:, 0, None, :] * grad_ext[:, :-2]
        + short_taps[:, 1, None, :] * grad_ext[:, 1:-1]
        + short_taps[:, 2, None, :] * grad_ext[:, 2:]
    )
    return (mixed, stream_grads.astype(jnp.bfloat16))


def solution(mesh):
    return jax.shard_map(
        on_device,
        mesh=mesh,
        in_specs=(
            P(None, "seq", "tp"),
            P(None, None, "tp"),
            P("seq", "tp"),
            P("tp"),
            P("tp", None),
            P("seq", None),
        ),
        out_specs=(P("seq", "tp"), P(None, "seq", "tp")),
        check_vma=False,
    )
```

```python
import functools
import math

import jax
import jax.numpy as jnp
import ml_dtypes
import numpy as np
from jax import lax
from jax.experimental import pallas as pl
from jax.experimental.pallas import tpu as pltpu
from jax.sharding import PartitionSpec as P


def passed_along(x, axis, by):
    devices = lax.axis_size(axis)
    pairs = [(i, i + by) for i in range(devices) if 0 <= i + by < devices]
    return lax.ppermute(x, axis, pairs)


def dft_tables(length):
    ids = np.arange(length)
    angles = (np.outer(ids, ids) % length) * (2.0 * math.pi / length)
    cosine, sine = np.cos(angles), np.sin(angles)
    table = np.block([[cosine, -sine], [sine, cosine]]).astype(np.float32)
    high = table.astype(ml_dtypes.bfloat16)
    low = (table - high.astype(np.float32)).astype(ml_dtypes.bfloat16)
    return high, low


def twiddle_table(devices, length):
    angles = -2.0 * math.pi * np.outer(np.arange(devices) + 0.25, np.arange(length)) / (devices * length)
    return np.stack([np.cos(angles), np.sin(angles)]).astype(np.float32)


def across_weights(devices):
    angles = -2.0 * math.pi * np.outer(np.arange(devices) + 0.25, np.arange(devices)) / devices
    return np.cos(angles), np.sin(angles)


def split_store(high_ref, low_ref, rows, lanes, value):
    high = value.astype(jnp.bfloat16)
    high_ref[rows, lanes] = high
    low_ref[rows, lanes] = (value - high.astype(jnp.float32)).astype(jnp.bfloat16)


row_step = 16
lane_step = 128


def tiles_of(channels, length, body):
    per_row = length // lane_step

    @pl.loop(0, (channels // row_step) * per_row)
    def _(step):
        row = pl.multiple_of((step // per_row) * row_step, row_step)
        lane = pl.multiple_of((step % per_row) * lane_step, lane_step)
        body(row, lane)


def complex_sum(values, real_weights, imag_weights):
    real = imag = None
    for value, real_w, imag_w in zip(values, real_weights, imag_weights):
        real_term, imag_term = value * float(real_w), value * float(imag_w)
        real = real_term if real is None else real + real_term
        imag = imag_term if imag is None else imag + imag_term
    return real, imag


def forward_across(x_ref, twiddle_ref, high_ref, low_ref):
    devices, channels, length = x_ref.shape
    half = devices // 2
    real_w, imag_w = across_weights(devices)

    def body(row, lane):
        lanes = pl.ds(lane, lane_step)
        upper = pl.ds(pl.multiple_of(length + lane, lane_step), lane_step)
        values = [x_ref[m, pl.ds(row, row_step), lanes].astype(jnp.float32) for m in range(devices)]
        for k in range(half):
            even = complex_sum(values[::2], real_w[k, ::2], imag_w[k, ::2])
            odd = complex_sum(values[1::2], real_w[k, 1::2], imag_w[k, 1::2])
            for at, real, imag in (
                (k, even[0] + odd[0], even[1] + odd[1]),
                (k + half, even[0] - odd[0], even[1] - odd[1]),
            ):
                twiddle_real = twiddle_ref[0, pl.ds(at, 1), lanes]
                twiddle_imag = twiddle_ref[1, pl.ds(at, 1), lanes]
                rows = pl.ds(pl.multiple_of(at * channels + row, row_step), row_step)
                split_store(high_ref, low_ref, rows, lanes, real * twiddle_real - imag * twiddle_imag)
                split_store(high_ref, low_ref, rows, upper, real * twiddle_imag + imag * twiddle_real)

    tiles_of(channels, length, body)


def transform(high_ref, low_ref, table_high_ref, table_low_ref, out_ref):
    width = out_ref.shape[1]
    part = 256

    @pl.loop(0, width // part)
    def _(step):
        lanes = pl.ds(pl.multiple_of(step * part, part), part)
        dot = functools.partial(jnp.dot, preferred_element_type=jnp.float32)
        out_ref[:, lanes] = (
            dot(high_ref[...], table_high_ref[:, lanes])
            + dot(low_ref[...], table_high_ref[:, lanes])
            + dot(high_ref[...], table_low_ref[:, lanes])
        )


def table_copies(table_refs, held_refs, sems):
    copies = [
        pltpu.make_async_copy(table, held, sems.at[i])
        for i, (table, held) in enumerate(zip(table_refs, held_refs))
    ]
    for copy in copies:
        copy.start()
    return copies


def spectrum_kernel(x_ref, twiddle_ref, table_high, table_low, out_ref, held_high, held_low, sems, high_ref, low_ref):
    copies = table_copies((table_high, table_low), (held_high, held_low), sems)
    forward_across(x_ref, twiddle_ref, high_ref, low_ref)
    for copy in copies:
        copy.wait()
    transform(high_ref, low_ref, held_high, held_low, out_ref)


def filter_kernel(
    sign, x_ref, twiddle_ref, table_high, table_low, spectrum_hbm, out_ref,
    held_high, held_low, spectrum_ref, sems, high_ref, low_ref, full_ref,
):
    devices, channels, length = x_ref.shape
    half = devices // 2
    copies = table_copies(
        (table_high, table_low, spectrum_hbm), (held_high, held_low, spectrum_ref), sems
    )
    forward_across(x_ref, twiddle_ref, high_ref, low_ref)
    for copy in copies:
        copy.wait()
    transform(high_ref, low_ref, held_high, held_low, full_ref)
    real_w, imag_w = across_weights(devices)
    scale = 1.0 / (devices * length)

    @pl.loop(0, devices * channels // row_step)
    def _(step):
        rows = pl.ds(pl.multiple_of(step * row_step, row_step), row_step)
        for lane in range(0, length, lane_step):
            lanes, upper = pl.ds(lane, lane_step), pl.ds(length + lane, lane_step)
            data_real, data_imag = full_ref[rows, lanes], full_ref[rows, upper]
            taps_real, taps_imag = spectrum_ref[rows, lanes], spectrum_ref[rows, upper] * sign
            split_store(high_ref, low_ref, rows, lanes, data_real * taps_real - data_imag * taps_imag)
            split_store(high_ref, low_ref, rows, upper, -(data_real * taps_imag + data_imag * taps_real))

    transform(high_ref, low_ref, held_high, held_low, full_ref)

    def inverse(row, lane):
        lanes = pl.ds(lane, lane_step)
        upper = pl.ds(pl.multiple_of(length + lane, lane_step), lane_step)
        sums = [None] * devices
        for k in range(half):
            turned = []
            for at in (k, k + half):
                rows = pl.ds(pl.multiple_of(at * channels + row, row_step), row_step)
                twiddle_real = twiddle_ref[0, pl.ds(at, 1), lanes]
                twiddle_imag = twiddle_ref[1, pl.ds(at, 1), lanes]
                real, imag = full_ref[rows, lanes], full_ref[rows, upper]
                turned.append((real * twiddle_real - imag * twiddle_imag, real * twiddle_imag + imag * twiddle_real))
            (near_real, near_imag), (far_real, far_imag) = turned
            even = (near_real + far_real, near_imag + far_imag)
            odd = (near_real - far_real, near_imag - far_imag)
            for m in range(devices):
                real, imag = odd if m % 2 else even
                term = real * float(scale * real_w[k, m]) - imag * float(scale * imag_w[k, m])
                sums[m] = term if sums[m] is None else sums[m] + term
        for m in range(devices):
            out_ref[m, pl.ds(row, row_step), lanes] = sums[m].astype(jnp.bfloat16)

    tiles_of(channels, length, inverse)


def tables_for(devices, length):
    high, low = dft_tables(length)
    return jnp.asarray(twiddle_table(devices, length)), jnp.asarray(high), jnp.asarray(low)


in_vmem = pl.BlockSpec(memory_space=pltpu.VMEM)
in_hbm = pl.BlockSpec(memory_space=pltpu.HBM)


def spectrum(x, tables):
    devices, channels, length = x.shape
    rows, width = devices * channels, 2 * length
    return pl.pallas_call(
        spectrum_kernel,
        out_shape=jax.ShapeDtypeStruct((rows, width), jnp.float32),
        in_specs=[in_vmem, in_vmem, in_hbm, in_hbm],
        out_specs=in_vmem,
        scratch_shapes=[pltpu.VMEM((width, width), jnp.bfloat16)] * 2
        + [pltpu.SemaphoreType.DMA((2,))]
        + [pltpu.VMEM((rows, width), jnp.bfloat16)] * 2,
        compiler_params=pltpu.CompilerParams(vmem_limit_bytes=58 << 20),
        cost_estimate=pl.CostEstimate(flops=6 * rows * width**2, bytes_accessed=8 << 20, transcendentals=0),
    )(x, *tables)


def filtered(x, taps_spectrum, tables, sign):
    devices, channels, length = x.shape
    rows, width = devices * channels, 2 * length
    return pl.pallas_call(
        functools.partial(filter_kernel, sign),
        out_shape=jax.ShapeDtypeStruct(x.shape, jnp.bfloat16),
        in_specs=[in_vmem, in_vmem, in_hbm, in_hbm, in_hbm],
        out_specs=in_vmem,
        scratch_shapes=[pltpu.VMEM((width, width), jnp.bfloat16)] * 2
        + [pltpu.VMEM((rows, width), jnp.float32), pltpu.SemaphoreType.DMA((3,))]
        + [pltpu.VMEM((rows, width), jnp.bfloat16)] * 2
        + [pltpu.VMEM((rows, width), jnp.float32)],
        compiler_params=pltpu.CompilerParams(vmem_limit_bytes=58 << 20),
        cost_estimate=pl.CostEstimate(flops=12 * rows * width**2, bytes_accessed=8 << 20, transcendentals=0),
    )(x, *tables, taps_spectrum)


def swapped(x, axis, bit):
    return lax.ppermute(x, axis, [(i, i ^ bit) for i in range(lax.axis_size(axis))])


def to_channels(turned):
    devices = lax.axis_size("seq")
    moved = lax.all_to_all(turned, "seq", split_axis=0, concat_axis=0, tiled=True)
    return moved.reshape(devices, turned.shape[0] // devices, turned.shape[1])


def turned_over(x):
    return x.astype(jnp.bfloat16).T


def to_positions(x):
    devices, channels, length = x.shape
    return lax.all_to_all(x.reshape(devices * channels, length), "seq", split_axis=0, concat_axis=0, tiled=True)


def on_device(streams, short_taps, filter_taps, skip_gain, w_out, cotangent):
    length = streams.shape[1]
    devices = lax.axis_size("seq")
    tables = tables_for(devices, length)
    taps_channels = to_channels(turned_over(filter_taps))
    previous = passed_along(streams[:, -2:, :], "seq", 1)
    extended = jnp.concatenate([previous, streams], axis=1).astype(jnp.float32)
    convolved = (
        short_taps[:, 0, None, :] * extended[:, 2:]
        + short_taps[:, 1, None, :] * extended[:, 1:-1]
        + short_taps[:, 2, None, :] * extended[:, :-2]
    )
    conv_q = convolved[0]
    conv_k = convolved[1]
    conv_v = convolved[2]
    source = conv_k * conv_v
    grad_gated = lax.dot_general(
        cotangent, w_out, (((1,), (1,)), ((), ())), preferred_element_type=jnp.float32
    )
    grad_state = grad_gated * conv_q
    shares = lax.axis_size("tp")
    place = lax.axis_index("tp")
    width = w_out.shape[1] // shares
    w_pieces = []
    for bits in range(shares):
        piece = lax.dynamic_slice_in_dim(w_out, (place ^ bits) * width, width, 1)
        w_pieces.append(swapped(piece, "tp", bits) if bits else piece)
    taps_spectrum = spectrum(taps_channels, tables)
    grad_turned, taps_spectrum = lax.optimization_barrier((turned_over(grad_state), taps_spectrum))
    early = 2 % shares
    source_channels, w_pieces[early] = lax.optimization_barrier(
        (to_channels(turned_over(source)), w_pieces[early])
    )
    state_channels = filtered(source_channels, taps_spectrum, tables, 1.0)
    state_channels, grad_received = lax.optimization_barrier((state_channels, to_channels(grad_turned)))
    grad_channels = filtered(grad_received, taps_spectrum, tables, -1.0)
    state_positions, grad_channels, w_pieces = lax.optimization_barrier(
        (to_positions(state_channels), grad_channels, w_pieces)
    )
    mixer_state = state_positions.T.astype(jnp.float32) + skip_gain * source
    gated = (conv_q * mixer_state).astype(jnp.bfloat16)
    pieces = {0: gated}
    bit = shares // 2
    while bit:
        order = sorted(pieces)
        received = swapped(jnp.stack([pieces[i] for i in order]), "tp", bit)
        pieces.update({i ^ bit: received[at] for at, i in enumerate(order)})
        bit //= 2
    total = sum(
        jnp.dot(pieces[i], w_pieces[i], preferred_element_type=jnp.float32) for i in range(shares)
    )
    mixed = total.astype(jnp.bfloat16)
    grad_q = grad_gated * mixer_state
    grad_positions, mixed = lax.optimization_barrier((to_positions(grad_channels), mixed))
    grad_source = grad_positions.T.astype(jnp.float32) + skip_gain * grad_state
    gradients = jnp.stack([grad_q, grad_source * conv_v, grad_source * conv_k])
    following = passed_along(gradients[:, :2, :], "seq", -1)
    grad_ext = jnp.concatenate([gradients, following], axis=1)
    stream_grads = (
        short_taps[:, 0, None, :] * grad_ext[:, :-2]
        + short_taps[:, 1, None, :] * grad_ext[:, 1:-1]
        + short_taps[:, 2, None, :] * grad_ext[:, 2:]
    )
    return (mixed, stream_grads.astype(jnp.bfloat16))


def solution(mesh):
    return jax.shard_map(
        on_device,
        mesh=mesh,
        in_specs=(
            P(None, "seq", "tp"),
            P(None, None, "tp"),
            P("seq", "tp"),
            P("tp"),
            P("tp", None),
            P("seq", None),
        ),
        out_specs=(P("seq", "tp"), P(None, "seq", "tp")),
        check_vma=False,
    )
```

```python
import functools
import math

import jax
import jax.numpy as jnp
import ml_dtypes
import numpy as np
from jax import lax
from jax.experimental import pallas as pl
from jax.experimental.pallas import tpu as pltpu
from jax.sharding import PartitionSpec as P


def passed_along(x, axis, by):
    devices = lax.axis_size(axis)
    pairs = [(i, i + by) for i in range(devices) if 0 <= i + by < devices]
    return lax.ppermute(x, axis, pairs)


def dft_tables(length):
    ids = np.arange(length)
    angles = (np.outer(ids, ids) % length) * (2.0 * math.pi / length)
    cosine, sine = np.cos(angles), np.sin(angles)
    table = np.block([[cosine, -sine], [sine, cosine]]).astype(np.float32)
    high = table.astype(ml_dtypes.bfloat16)
    low = (table - high.astype(np.float32)).astype(ml_dtypes.bfloat16)
    return high, low


def twiddle_table(devices, length):
    angles = -2.0 * math.pi * np.outer(np.arange(devices) + 0.25, np.arange(length)) / (devices * length)
    return np.stack([np.cos(angles), np.sin(angles)]).astype(np.float32)


def across_weights(devices):
    angles = -2.0 * math.pi * np.outer(np.arange(devices) + 0.25, np.arange(devices)) / devices
    return np.cos(angles), np.sin(angles)


def split_store(high_ref, low_ref, rows, lanes, value):
    high = value.astype(jnp.bfloat16)
    high_ref[rows, lanes] = high
    low_ref[rows, lanes] = (value - high.astype(jnp.float32)).astype(jnp.bfloat16)


row_step = 16
lane_step = 128


def tiles_of(channels, length, body):
    per_row = length // lane_step

    @pl.loop(0, (channels // row_step) * per_row)
    def _(step):
        row = pl.multiple_of((step // per_row) * row_step, row_step)
        lane = pl.multiple_of((step % per_row) * lane_step, lane_step)
        body(row, lane)


def complex_sum(values, real_weights, imag_weights):
    real = imag = None
    for value, real_w, imag_w in zip(values, real_weights, imag_weights):
        real_term, imag_term = value * float(real_w), value * float(imag_w)
        real = real_term if real is None else real + real_term
        imag = imag_term if imag is None else imag + imag_term
    return real, imag


def forward_across(x_ref, twiddle_ref, high_ref, low_ref):
    devices, channels, length = x_ref.shape
    half = devices // 2
    real_w, imag_w = across_weights(devices)

    def body(row, lane):
        lanes = pl.ds(lane, lane_step)
        upper = pl.ds(pl.multiple_of(length + lane, lane_step), lane_step)
        values = [x_ref[m, pl.ds(row, row_step), lanes].astype(jnp.float32) for m in range(devices)]
        for k in range(half):
            even = complex_sum(values[::2], real_w[k, ::2], imag_w[k, ::2])
            odd = complex_sum(values[1::2], real_w[k, 1::2], imag_w[k, 1::2])
            for at, real, imag in (
                (k, even[0] + odd[0], even[1] + odd[1]),
                (k + half, even[0] - odd[0], even[1] - odd[1]),
            ):
                twiddle_real = twiddle_ref[0, pl.ds(at, 1), lanes]
                twiddle_imag = twiddle_ref[1, pl.ds(at, 1), lanes]
                rows = pl.ds(pl.multiple_of(at * channels + row, row_step), row_step)
                split_store(high_ref, low_ref, rows, lanes, real * twiddle_real - imag * twiddle_imag)
                split_store(high_ref, low_ref, rows, upper, real * twiddle_imag + imag * twiddle_real)

    tiles_of(channels, length, body)


def transform(high_ref, low_ref, table_high_ref, table_low_ref, out_ref):
    width = out_ref.shape[1]
    part = 256

    @pl.loop(0, width // part)
    def _(step):
        lanes = pl.ds(pl.multiple_of(step * part, part), part)
        dot = functools.partial(jnp.dot, preferred_element_type=jnp.float32)
        out_ref[:, lanes] = (
            dot(high_ref[...], table_high_ref[:, lanes])
            + dot(low_ref[...], table_high_ref[:, lanes])
            + dot(high_ref[...], table_low_ref[:, lanes])
        )


def table_copies(table_refs, held_refs, sems):
    copies = [
        pltpu.make_async_copy(table, held, sems.at[i])
        for i, (table, held) in enumerate(zip(table_refs, held_refs))
    ]
    for copy in copies:
        copy.start()
    return copies


def spectrum_kernel(x_ref, twiddle_ref, table_high, table_low, out_ref, held_high, held_low, sems, high_ref, low_ref):
    copies = table_copies((table_high, table_low), (held_high, held_low), sems)
    forward_across(x_ref, twiddle_ref, high_ref, low_ref)
    for copy in copies:
        copy.wait()
    transform(high_ref, low_ref, held_high, held_low, out_ref)


def filter_kernel(
    sign, x_ref, twiddle_ref, table_high, table_low, spectrum_hbm, out_ref,
    held_high, held_low, spectrum_ref, sems, high_ref, low_ref, full_ref,
):
    devices, channels, length = x_ref.shape
    half = devices // 2
    copies = table_copies(
        (table_high, table_low, spectrum_hbm), (held_high, held_low, spectrum_ref), sems
    )
    forward_across(x_ref, twiddle_ref, high_ref, low_ref)
    for copy in copies:
        copy.wait()
    transform(high_ref, low_ref, held_high, held_low, full_ref)
    real_w, imag_w = across_weights(devices)
    scale = 1.0 / (devices * length)

    @pl.loop(0, devices * channels // row_step)
    def _(step):
        rows = pl.ds(pl.multiple_of(step * row_step, row_step), row_step)
        for lane in range(0, length, lane_step):
            lanes, upper = pl.ds(lane, lane_step), pl.ds(length + lane, lane_step)
            data_real, data_imag = full_ref[rows, lanes], full_ref[rows, upper]
            taps_real, taps_imag = spectrum_ref[rows, lanes], spectrum_ref[rows, upper] * sign
            split_store(high_ref, low_ref, rows, lanes, data_real * taps_real - data_imag * taps_imag)
            split_store(high_ref, low_ref, rows, upper, -(data_real * taps_imag + data_imag * taps_real))

    transform(high_ref, low_ref, held_high, held_low, full_ref)

    def inverse(row, lane):
        lanes = pl.ds(lane, lane_step)
        upper = pl.ds(pl.multiple_of(length + lane, lane_step), lane_step)
        sums = [None] * devices
        for k in range(half):
            turned = []
            for at in (k, k + half):
                rows = pl.ds(pl.multiple_of(at * channels + row, row_step), row_step)
                twiddle_real = twiddle_ref[0, pl.ds(at, 1), lanes]
                twiddle_imag = twiddle_ref[1, pl.ds(at, 1), lanes]
                real, imag = full_ref[rows, lanes], full_ref[rows, upper]
                turned.append((real * twiddle_real - imag * twiddle_imag, real * twiddle_imag + imag * twiddle_real))
            (near_real, near_imag), (far_real, far_imag) = turned
            even = (near_real + far_real, near_imag + far_imag)
            odd = (near_real - far_real, near_imag - far_imag)
            for m in range(devices):
                real, imag = odd if m % 2 else even
                term = real * float(scale * real_w[k, m]) - imag * float(scale * imag_w[k, m])
                sums[m] = term if sums[m] is None else sums[m] + term
        for m in range(devices):
            out_ref[m, pl.ds(row, row_step), lanes] = sums[m].astype(jnp.bfloat16)

    tiles_of(channels, length, inverse)


def tables_for(devices, length):
    high, low = dft_tables(length)
    return jnp.asarray(twiddle_table(devices, length)), jnp.asarray(high), jnp.asarray(low)


in_vmem = pl.BlockSpec(memory_space=pltpu.VMEM)
in_hbm = pl.BlockSpec(memory_space=pltpu.HBM)


def spectrum(x, tables):
    devices, channels, length = x.shape
    rows, width = devices * channels, 2 * length
    return pl.pallas_call(
        spectrum_kernel,
        out_shape=jax.ShapeDtypeStruct((rows, width), jnp.float32),
        in_specs=[in_vmem, in_vmem, in_hbm, in_hbm],
        out_specs=in_vmem,
        scratch_shapes=[pltpu.VMEM((width, width), jnp.bfloat16)] * 2
        + [pltpu.SemaphoreType.DMA((2,))]
        + [pltpu.VMEM((rows, width), jnp.bfloat16)] * 2,
        compiler_params=pltpu.CompilerParams(vmem_limit_bytes=58 << 20),
        cost_estimate=pl.CostEstimate(flops=6 * rows * width**2, bytes_accessed=8 << 20, transcendentals=0),
    )(x, *tables)


def filtered(x, taps_spectrum, tables, sign):
    devices, channels, length = x.shape
    rows, width = devices * channels, 2 * length
    return pl.pallas_call(
        functools.partial(filter_kernel, sign),
        out_shape=jax.ShapeDtypeStruct(x.shape, jnp.bfloat16),
        in_specs=[in_vmem, in_vmem, in_hbm, in_hbm, in_hbm],
        out_specs=in_vmem,
        scratch_shapes=[pltpu.VMEM((width, width), jnp.bfloat16)] * 2
        + [pltpu.VMEM((rows, width), jnp.float32), pltpu.SemaphoreType.DMA((3,))]
        + [pltpu.VMEM((rows, width), jnp.bfloat16)] * 2
        + [pltpu.VMEM((rows, width), jnp.float32)],
        compiler_params=pltpu.CompilerParams(vmem_limit_bytes=58 << 20),
        cost_estimate=pl.CostEstimate(flops=12 * rows * width**2, bytes_accessed=8 << 20, transcendentals=0),
    )(x, *tables, taps_spectrum)


def swapped(x, axis, bit):
    return lax.ppermute(x, axis, [(i, i ^ bit) for i in range(lax.axis_size(axis))])


def to_channels(turned):
    devices = lax.axis_size("seq")
    moved = lax.all_to_all(turned, "seq", split_axis=0, concat_axis=0, tiled=True)
    return moved.reshape(devices, turned.shape[0] // devices, turned.shape[1])


def turned_over(x):
    return x.astype(jnp.bfloat16).T


def to_positions(x):
    devices, channels, length = x.shape
    return lax.all_to_all(x.reshape(devices * channels, length), "seq", split_axis=0, concat_axis=0, tiled=True)


def on_device(streams, short_taps, filter_taps, skip_gain, w_out, cotangent):
    length = streams.shape[1]
    devices = lax.axis_size("seq")
    tables = tables_for(devices, length)
    taps_channels = to_channels(turned_over(filter_taps))
    previous = passed_along(streams[:, -2:, :], "seq", 1)
    extended = jnp.concatenate([previous, streams], axis=1).astype(jnp.float32)
    convolved = (
        short_taps[:, 0, None, :] * extended[:, 2:]
        + short_taps[:, 1, None, :] * extended[:, 1:-1]
        + short_taps[:, 2, None, :] * extended[:, :-2]
    )
    conv_q = convolved[0]
    conv_k = convolved[1]
    conv_v = convolved[2]
    source = conv_k * conv_v
    grad_gated = lax.dot_general(
        cotangent, w_out, (((1,), (1,)), ((), ())), preferred_element_type=jnp.float32
    )
    grad_state = grad_gated * conv_q
    shares = lax.axis_size("tp")
    place = lax.axis_index("tp")
    width = w_out.shape[1] // shares
    w_pieces = []
    for bits in range(shares):
        piece = lax.dynamic_slice_in_dim(w_out, (place ^ bits) * width, width, 1)
        w_pieces.append(swapped(piece, "tp", bits) if bits else piece)
    taps_spectrum = spectrum(taps_channels, tables)
    grad_turned, taps_spectrum = lax.optimization_barrier((turned_over(grad_state), taps_spectrum))
    early = 2 % shares
    source_channels = to_channels(turned_over(source))
    state_channels = filtered(source_channels, taps_spectrum, tables, 1.0)
    state_channels, grad_received, w_pieces[early] = lax.optimization_barrier(
        (state_channels, to_channels(grad_turned), w_pieces[early])
    )
    grad_channels = filtered(grad_received, taps_spectrum, tables, -1.0)
    state_positions, grad_channels, w_pieces = lax.optimization_barrier(
        (to_positions(state_channels), grad_channels, w_pieces)
    )
    mixer_state = state_positions.T.astype(jnp.float32) + skip_gain * source
    gated = (conv_q * mixer_state).astype(jnp.bfloat16)
    pieces = {0: gated}
    bit = shares // 2
    while bit:
        order = sorted(pieces)
        if bit == 1:
            grad_positions, pieces = lax.optimization_barrier((to_positions(grad_channels), pieces))
        received = swapped(jnp.stack([pieces[i] for i in order]), "tp", bit)
        pieces.update({i ^ bit: received[at] for at, i in enumerate(order)})
        bit //= 2
    total = sum(
        jnp.dot(pieces[i], w_pieces[i], preferred_element_type=jnp.float32) for i in range(shares)
    )
    mixed = total.astype(jnp.bfloat16)
    grad_q = grad_gated * mixer_state
    grad_source = grad_positions.T.astype(jnp.float32) + skip_gain * grad_state
    gradients = jnp.stack([grad_q, grad_source * conv_v, grad_source * conv_k])
    following = passed_along(gradients[:, :2, :], "seq", -1)
    grad_ext = jnp.concatenate([gradients, following], axis=1)
    stream_grads = (
        short_taps[:, 0, None, :] * grad_ext[:, :-2]
        + short_taps[:, 1, None, :] * grad_ext[:, 1:-1]
        + short_taps[:, 2, None, :] * grad_ext[:, 2:]
    )
    return (mixed, stream_grads.astype(jnp.bfloat16))


def solution(mesh):
    return jax.shard_map(
        on_device,
        mesh=mesh,
        in_specs=(
            P(None, "seq", "tp"),
            P(None, None, "tp"),
            P("seq", "tp"),
            P("tp"),
            P("tp", None),
            P("seq", None),
        ),
        out_specs=(P("seq", "tp"), P(None, "seq", "tp")),
        check_vma=False,
    )
```
